32 devices in a mesh: grp: 2 (over x), row: 8 (over z, y), col: 2 (over core).
Axes of the slice: x: 2, y: 2, z: 4, core: 2. Of those that a mesh axis runs over, the one named last changes fastest.
Arguments:
- alignment_activations: bfloat16 [2, 64, 128, 256], P(None, ('grp', 'row')), parts along dimension 1, may hold values from -6 to 6
- first_projection_matrix: bfloat16 [2, 256, 32], replicated, may hold values from -0.375 to 0.375
- second_projection_matrix: bfloat16 [2, 256, 32], replicated, may hold values from -0.375 to 0.375
- final_projection_matrix: bfloat16 [2, 1024, 128], replicated, may hold values from -1 to 1
- final_offset_vector: float32 [2, 128], replicated, may hold values from -3 to 3
Outputs:
- update: bfloat16 [2, 256, 128, 128], P(None, ('grp', 'row'), 'col'), parts along dimension 1
The draws below stay inside these ranges and needn't reach their ends.
There are 2 independent parts, one for each index of `grp`. The reference program is written for one: setup_inputs(seed, part) draws one part's arguments, and reference() takes and returns one part's arrays. A program takes and returns all parts, laid end to end along the dimension named above; an argument that names none is the same for every part. Nothing has to cross between parts.
All inputs are finite; a program needn't handle non-finite values.
Results may differ from the reference program's by a relative error of at most 0.007.
Values may be sent and summed in bfloat16 or wider, within the bound.
A program may use at most 128 MiB of HBM per device.

```python
import jax
import jax.numpy as jnp
from jax import lax

ALIGN_FEATURES = 256
PROJECTED_WIDTH = 32
PAIR_FEATURES = 128
LAYERS = 2
ALIGNED_SEQS = 32
SEQUENCE_LENGTH = 128


def shard_levels(key, extent, cuts, low, largest):
    def one(dim, parts):
        steps = jax.random.uniform(jax.random.fold_in(jax.random.fold_in(key, 6), dim), (parts,), jnp.float32, low / len(cuts), largest / len(cuts))
        return jnp.repeat(jnp.exp(steps), extent[dim] // parts).reshape((-1,) + (1,) * (len(extent) - dim - 1))

    loudness = one(*cuts[0])
    for cut in cuts[1:]:
        loudness = loudness * one(*cut)
    return loudness


def normal_values(key, dims, spread, bound, pieces=(), kind=jnp.bfloat16):
    values = spread * jax.random.normal(key, dims, jnp.float32)
    if pieces:
        values = values * shard_levels(key, dims, pieces, -0.22, 0.18)
    return jnp.clip(values, -bound, bound).astype(kind)


def setup_inputs(seed: int = 0, part: int = 0) -> dict:
    key_of = jax.random.split(jax.random.key(seed), 6)
    own_keys = jax.random.split(jax.random.fold_in(key_of[5], part), 6)
    alignment_activations = normal_values(own_keys[0], (LAYERS, ALIGNED_SEQS, SEQUENCE_LENGTH, ALIGN_FEATURES), 1.0, 6.0, ((1, 8),))
    first_projection_matrix = normal_values(key_of[1], (LAYERS, ALIGN_FEATURES, PROJECTED_WIDTH), ALIGN_FEATURES ** -0.5, 0.375)
    second_projection_matrix = normal_values(key_of[2], (LAYERS, ALIGN_FEATURES, PROJECTED_WIDTH), ALIGN_FEATURES ** -0.5, 0.375)
    final_projection_matrix = normal_values(key_of[3], (LAYERS, PROJECTED_WIDTH * PROJECTED_WIDTH, PAIR_FEATURES), (max(1, PROJECTED_WIDTH * PROJECTED_WIDTH // ALIGNED_SEQS)) ** -0.5, 1.0)
    final_offset_vector = normal_values(key_of[4], (LAYERS, PAIR_FEATURES), 0.5, 3.0, (), jnp.float32)
    return {"alignment_activations": alignment_activations, "first_projection_matrix": first_projection_matrix, "second_projection_matrix": second_projection_matrix, "final_projection_matrix": final_projection_matrix, "final_offset_vector": final_offset_vector}


def one_block(activations, first_matrix, second_matrix, final_matrix, offset_vector):
    entry_lines = activations.astype(jnp.float32)
    average = lax.optimization_barrier(jnp.mean(entry_lines, axis=-1, keepdims=True))
    centred = entry_lines - average
    variance = lax.optimization_barrier(jnp.mean(centred * centred, axis=-1, keepdims=True))
    standardized = (centred * lax.rsqrt(variance + 1e-05)).astype(jnp.bfloat16)
    unrolled_products = standardized.reshape(ALIGNED_SEQS * SEQUENCE_LENGTH, ALIGN_FEATURES)
    first_factor = jnp.dot(unrolled_products, first_matrix, preferred_element_type=jnp.float32).astype(jnp.bfloat16).reshape(ALIGNED_SEQS, SEQUENCE_LENGTH, PROJECTED_WIDTH)
    second_factor = jnp.dot(unrolled_products, second_matrix, preferred_element_type=jnp.float32).astype(jnp.bfloat16).reshape(ALIGNED_SEQS, SEQUENCE_LENGTH, PROJECTED_WIDTH)
    right_wide = second_factor.astype(jnp.float32)
    block_rows = min(SEQUENCE_LENGTH, 16)
    reciprocal = 1.0 / ALIGNED_SEQS

    def tile_block(offset):
        left_block = lax.dynamic_slice_in_dim(first_factor, offset, block_rows, 1).astype(jnp.float32)
        products = jnp.einsum('sic,sjd->ijcd', left_block, right_wide) * reciprocal
        products = products.astype(jnp.bfloat16).reshape(block_rows * SEQUENCE_LENGTH, PROJECTED_WIDTH * PROJECTED_WIDTH)
        projected = jnp.dot(products, final_matrix, preferred_element_type=jnp.float32) + offset_vector
        return projected.astype(jnp.bfloat16).reshape(block_rows, SEQUENCE_LENGTH, PAIR_FEATURES)
    starts = jnp.arange(SEQUENCE_LENGTH // block_rows, dtype=jnp.int32) * block_rows
    return lax.map(tile_block, starts).reshape(SEQUENCE_LENGTH, SEQUENCE_LENGTH, PAIR_FEATURES)

def reference(alignment_activations, first_projection_matrix, second_projection_matrix, final_projection_matrix, final_offset_vector):
    results = []
    for layer in range(LAYERS):
        results.append(one_block(alignment_activations[layer], first_projection_matrix[layer], second_projection_matrix[layer], final_projection_matrix[layer], final_offset_vector[layer]))
    return jnp.stack(results, axis=0)
```

```python
import functools

import jax
import jax.numpy as jnp
from jax import lax
from jax.experimental import pallas as pl
from jax.experimental.pallas import tpu as pltpu
from jax.sharding import PartitionSpec as P

LANES = 128
VMEM_BUDGET = 48 * 1024 * 1024


def standardize_features(activations):
    entry_lines = activations.astype(jnp.float32)
    average = jnp.mean(entry_lines, axis=-1, keepdims=True)
    centred = entry_lines - average
    variance = jnp.mean(centred * centred, axis=-1, keepdims=True)
    return (centred * lax.rsqrt(variance + 1e-05)).astype(jnp.bfloat16)


def pair_tiles(left_tile, right_tile, final_matrix, offset_vector):
    depth_all = left_tile.shape[0]
    tile_rows = left_tile.shape[1]
    tile_cols = right_tile.shape[1]
    hidden = left_tile.shape[2]
    pair_width = final_matrix.shape[1]
    block_rows = max(1, min(tile_rows, 2048 // tile_cols))
    reciprocal = 1.0 / depth_all

    def tile_block(offset):
        left_block = lax.dynamic_slice_in_dim(left_tile, offset, block_rows, 1)
        products = (
            jnp.einsum("sic,sjd->ijcd", left_block, right_tile, preferred_element_type=jnp.float32)
            * reciprocal
        )
        products = products.astype(jnp.bfloat16).reshape(block_rows * tile_cols, hidden * hidden)
        projected = (
            jnp.dot(products, final_matrix, preferred_element_type=jnp.float32) + offset_vector
        )
        return projected.astype(jnp.bfloat16).reshape(block_rows, tile_cols, pair_width)

    starts = jnp.arange(tile_rows // block_rows, dtype=jnp.int32) * block_rows
    return lax.map(tile_block, starts).reshape(tile_rows, tile_cols, pair_width)


def block_update(activations, first_matrix, second_matrix, final_matrix, offset_vector):
    local_sequences, sequence_positions, feature_number = activations.shape
    row_count = lax.axis_size("row")
    col_count = lax.axis_size("col")
    row_block = sequence_positions // row_count
    col_block = sequence_positions // col_count
    hidden = first_matrix.shape[1]
    unrolled_products = standardize_features(activations).reshape(
        local_sequences * sequence_positions, feature_number
    )
    first_factor = jnp.dot(
        unrolled_products, first_matrix, preferred_element_type=jnp.float32
    ).astype(jnp.bfloat16)
    second_factor = jnp.dot(
        unrolled_products, second_matrix, preferred_element_type=jnp.float32
    ).astype(jnp.bfloat16)
    col_place = lax.axis_index("col")
    halves = second_factor.reshape(local_sequences, col_count, col_block * hidden)
    own_half = lax.dynamic_index_in_dim(halves, col_place, 1, keepdims=False)
    left_send = first_factor.reshape(local_sequences, row_count, row_block * hidden)
    left_got = lax.all_to_all(left_send, "row", split_axis=1, concat_axis=0, tiled=True)
    left_tile = left_got.reshape(-1, row_block, hidden)
    panel = lax.all_gather(own_half, "row", axis=0, tiled=True)
    right_tile = panel.reshape(-1, col_block, hidden)
    return pair_tiles(left_tile, right_tile, final_matrix, offset_vector)


def collective_body(activations, first_matrix, second_matrix, final_matrix, offsets):
    results = []
    for layer in range(activations.shape[0]):
        results.append(
            block_update(
                activations[layer],
                first_matrix[layer],
                second_matrix[layer],
                final_matrix[layer],
                offsets[layer],
            )
        )
    return jnp.stack(results, axis=0)


def dot32(a, b):
    return jnp.dot(a, b, preferred_element_type=jnp.float32)


def dot32_nt(a, b):
    return lax.dot_general(a, b, (((1,), (1,)), ((), ())), preferred_element_type=jnp.float32)


def opm_kernel(
    n,
    x_hbm,
    w1_ref,
    w2_ref,
    wf_hbm,
    b_ref,
    out_hbm,
    x_ref,
    wf_ref,
    normed,
    left_send,
    right_send,
    left_got,
    right_got,
    wide,
    w_rows,
    left_rows,
    right_rows,
    half_done,
    out_ref,
    in_sem,
    out_sem,
    left_ssem,
    left_rsem,
    right_ssem,
    right_rsem,
):
    layers, seqs, positions, _ = x_ref.shape
    hidden = w1_ref.shape[2]
    row_block, col_block = out_ref.shape[1], out_ref.shape[2]
    depth = n * seqs
    pairs = seqs // 2
    me = lax.axis_index("row")
    col = lax.axis_index("col")

    fetches = []
    for layer in range(layers):
        fetches.append(pltpu.make_async_copy(x_hbm.at[layer], x_ref.at[layer], in_sem.at[layer]))
    fetches.append(pltpu.make_async_copy(wf_hbm, wf_ref, in_sem.at[layers]))
    for fetch in fetches:
        fetch.start()

    barrier = pltpu.get_barrier_semaphore()
    for step in range(1, n):
        pl.semaphore_signal(
            barrier,
            inc=1,
            device_id={"row": lax.rem(me + step, n)},
            device_id_type=pl.DeviceIdType.MESH,
        )

    spread = (
        lax.broadcasted_iota(jnp.int32, (hidden, LANES), 1) % hidden
        == lax.broadcasted_iota(jnp.int32, (hidden, LANES), 0)
    ).astype(jnp.bfloat16)
    same = (
        lax.broadcasted_iota(jnp.int32, (hidden, hidden), 1)
        == lax.broadcasted_iota(jnp.int32, (hidden, hidden), 0)
    ).astype(jnp.bfloat16)

    copies = []
    for layer in range(layers):
        fetches[layer].wait()
        w1_wide = dot32(w1_ref[layer], spread).astype(jnp.bfloat16)
        w2_turned = dot32_nt(same, w2_ref[layer]).astype(jnp.bfloat16)
        lane = lax.broadcasted_iota(jnp.int32, (positions, LANES), 1)
        packed = jnp.zeros((positions, LANES), jnp.float32)
        for s in range(seqs):
            entry = standardize_features(x_ref[layer, s])
            normed[s] = entry
            group = (lane >= s * hidden) & (lane < (s + 1) * hidden)
            packed = jnp.where(group, dot32(entry, w1_wide), packed)
        left_send[layer] = packed.astype(jnp.bfloat16)
        mine = pl.ds(pl.multiple_of(col * col_block, col_block), col_block)
        for low in range(pairs):
            both = jnp.concatenate([normed[low, mine, :], normed[low + pairs, mine, :]], axis=0)
            right = dot32_nt(w2_turned, both).astype(jnp.bfloat16)
            right_send[layer, low * hidden : (low + 1) * hidden, :] = right
        own_rows = pl.ds(pl.multiple_of(me * row_block, row_block), row_block)
        left_got[layer, me] = left_send[layer, own_rows, :]
        right_got[layer, me] = right_send[layer]
        if layer == 0:
            pl.semaphore_wait(barrier, n - 1)
        for step in range(1, n):
            to = lax.rem(me + step, n)
            their_rows = pl.ds(pl.multiple_of(to * row_block, row_block), row_block)
            left_copy = pltpu.make_async_remote_copy(
                src_ref=left_send.at[layer, their_rows, :],
                dst_ref=left_got.at[layer, me],
                send_sem=left_ssem.at[layer, step],
                recv_sem=left_rsem.at[layer, me],
                device_id={"row": to},
                device_id_type=pl.DeviceIdType.MESH,
            )
            right_copy = pltpu.make_async_remote_copy(
                src_ref=right_send.at[layer],
                dst_ref=right_got.at[layer, me],
                send_sem=right_ssem.at[layer, step],
                recv_sem=right_rsem.at[layer, me],
                device_id={"row": to},
                device_id_type=pl.DeviceIdType.MESH,
            )
            left_copy.start()
            right_copy.start()
            copies.extend([left_copy, right_copy])

    fetches[layers].wait()
    for layer in range(layers):
        wide[...] = wf_ref[layer].astype(jnp.float32)
        for d in range(hidden):
            piece = wide[pl.ds(d, hidden, stride=hidden), :].astype(jnp.bfloat16)
            for s in range(seqs):
                w_rows[layer, s * hidden : (s + 1) * hidden, d * LANES : (d + 1) * LANES] = piece

    lane = lax.broadcasted_iota(jnp.int32, (row_block, LANES), 1)
    stores = []
    for layer in range(layers):
        for step in range(1, n):
            source = lax.rem(me + n - step, n)
            pltpu.make_async_remote_copy(
                src_ref=left_got.at[layer, source],
                dst_ref=left_got.at[layer, source],
                send_sem=left_ssem.at[layer, step],
                recv_sem=left_rsem.at[layer, source],
                device_id={"row": source},
                device_id_type=pl.DeviceIdType.MESH,
            ).wait_recv()
        for r in range(n):
            block = left_got[layer, r].astype(jnp.float32)
            for s in range(seqs):
                group = (lane >= s * hidden) & (lane < (s + 1) * hidden)
                left_rows[pl.ds(r * seqs + s, row_block, stride=depth), :] = jnp.where(
                    group, block, 0.0
                )
        left_all = left_rows[...].astype(jnp.bfloat16)
        for d in range(0, hidden, 2):
            two = dot32(left_all, w_rows[layer, :, d * LANES : (d + 2) * LANES])
            two = two.astype(jnp.bfloat16)
            for k in range(2):
                for i in range(row_block):
                    half_done[
                        (d + k) * depth : (d + k + 1) * depth, i * LANES : (i + 1) * LANES
                    ] = two[i * depth : (i + 1) * depth, k * LANES : (k + 1) * LANES]

        for step in range(1, n):
            source = lax.rem(me + n - step, n)
            pltpu.make_async_remote_copy(
                src_ref=right_got.at[layer, source],
                dst_ref=right_got.at[layer, source],
                send_sem=right_ssem.at[layer, step],
                recv_sem=right_rsem.at[layer, source],
                device_id={"row": source},
                device_id_type=pl.DeviceIdType.MESH,
            ).wait_recv()
        for r in range(n):
            for low in range(pairs):
                block = right_got[layer, r, low * hidden : (low + 1) * hidden, :]
                block = block.astype(jnp.float32)
                right_rows[pl.ds(r * seqs + low, hidden, stride=depth), :] = block
                right_rows[pl.ds(r * seqs + low + pairs, hidden, stride=depth), :] = pltpu.roll(
                    block, col_block, 1
                )
        right_all = right_rows[...].T[:col_block].astype(jnp.bfloat16)
        scale = 1.0 / depth
        for i in range(0, row_block, 2):
            two = dot32(right_all, half_done[:, i * LANES : (i + 2) * LANES]) * scale
            for k in range(2):
                done = two[:, k * LANES : (k + 1) * LANES] + b_ref[layer : layer + 1, :]
                out_ref[layer, i + k] = done.astype(jnp.bfloat16)
        store = pltpu.make_async_copy(out_ref.at[layer], out_hbm.at[layer], out_sem.at[layer])
        store.start()
        stores.append(store)

    for copy in copies:
        copy.wait_send()
    for store in stores:
        store.wait()


def kernel_fits(n, cols, x_shape, hidden, pair_width):
    layers, seqs, positions, features = x_shape
    row_block, col_block = positions // n, positions // cols
    depth = n * seqs
    need = 4 * layers * seqs * positions * features + 4 * depth * hidden * row_block * pair_width
    return (
        seqs * hidden == LANES
        and seqs % 2 == 0
        and 2 * col_block == LANES
        and pair_width == LANES
        and row_block % 16 == 0
        and depth % 16 == 0
        and n > 1
        and need < VMEM_BUDGET
    )


def kernel_body(n, cols, x, w1, w2, wf, b):
    layers, seqs, positions, features = x.shape
    hidden = w1.shape[2]
    pair_width = wf.shape[2]
    row_block, col_block = positions // n, positions // cols
    depth = n * seqs
    packed = (seqs // 2) * hidden
    bf16, f32 = jnp.bfloat16, jnp.float32
    vmem = pl.BlockSpec(memory_space=pltpu.VMEM)
    anywhere = pl.BlockSpec(memory_space=pl.ANY)
    out_shape = (layers, row_block, col_block, pair_width)
    return pl.pallas_call(
        functools.partial(opm_kernel, n),
        out_shape=jax.ShapeDtypeStruct(out_shape, bf16),
        in_specs=[anywhere, vmem, vmem, anywhere, vmem],
        out_specs=anywhere,
        scratch_shapes=[
            pltpu.VMEM(x.shape, bf16),
            pltpu.VMEM(wf.shape, bf16),
            pltpu.VMEM((seqs, positions, features), bf16),
            pltpu.VMEM((layers, positions, LANES), bf16),
            pltpu.VMEM((layers, packed, LANES), bf16),
            pltpu.VMEM((layers, n, row_block, LANES), bf16),
            pltpu.VMEM((layers, n, packed, LANES), bf16),
            pltpu.VMEM((hidden * hidden, pair_width), f32),
            pltpu.VMEM((layers, LANES, hidden * pair_width), bf16),
            pltpu.VMEM((row_block * depth, LANES), f32),
            pltpu.VMEM((hidden * depth, LANES), f32),
            pltpu.VMEM((hidden * depth, row_block * pair_width), bf16),
            pltpu.VMEM(out_shape, bf16),
            pltpu.SemaphoreType.DMA((layers + 1,)),
            pltpu.SemaphoreType.DMA((layers,)),
            pltpu.SemaphoreType.DMA((layers, n)),
            pltpu.SemaphoreType.DMA((layers, n)),
            pltpu.SemaphoreType.DMA((layers, n)),
            pltpu.SemaphoreType.DMA((layers, n)),
        ],
        compiler_params=pltpu.CompilerParams(
            collective_id=0, has_side_effects=True, vmem_limit_bytes=VMEM_BUDGET
        ),
        name="outer_product_mean",
    )(x, w1, w2, wf, b)


def solution(mesh):
    n, cols = mesh.shape["row"], mesh.shape["col"]

    def body(x, w1, w2, wf, b):
        if kernel_fits(n, cols, x.shape, w1.shape[2], wf.shape[2]):
            return kernel_body(n, cols, x, w1, w2, wf, b)
        return collective_body(x, w1, w2, wf, b)

    in_specs = (P(None, ("grp", "row"), None, None), P(), P(), P(), P())
    out_specs = P(None, ("grp", "row"), "col", None)
    return jax.shard_map(body, mesh=mesh, in_specs=in_specs, out_specs=out_specs, check_vma=False)
```

```python
import functools

import jax
import jax.numpy as jnp
from jax import lax
from jax.experimental import pallas as pl
from jax.experimental.pallas import tpu as pltpu
from jax.sharding import PartitionSpec as P

LANES = 128
VMEM_BUDGET = 63 * 1024 * 1024


def standardize_features(activations):
    entry_lines = activations.astype(jnp.float32)
    average = jnp.mean(entry_lines, axis=-1, keepdims=True)
    centred = entry_lines - average
    variance = jnp.mean(centred * centred, axis=-1, keepdims=True)
    return (centred * lax.rsqrt(variance + 1e-05)).astype(jnp.bfloat16)


def pair_tiles(left_tile, right_tile, final_matrix, offset_vector):
    depth_all = left_tile.shape[0]
    tile_rows = left_tile.shape[1]
    tile_cols = right_tile.shape[1]
    hidden = left_tile.shape[2]
    pair_width = final_matrix.shape[1]
    block_rows = max(1, min(tile_rows, 2048 // tile_cols))
    reciprocal = 1.0 / depth_all

    def tile_block(offset):
        left_block = lax.dynamic_slice_in_dim(left_tile, offset, block_rows, 1)
        products = (
            jnp.einsum("sic,sjd->ijcd", left_block, right_tile, preferred_element_type=jnp.float32)
            * reciprocal
        )
        products = products.astype(jnp.bfloat16).reshape(block_rows * tile_cols, hidden * hidden)
        projected = (
            jnp.dot(products, final_matrix, preferred_element_type=jnp.float32) + offset_vector
        )
        return projected.astype(jnp.bfloat16).reshape(block_rows, tile_cols, pair_width)

    starts = jnp.arange(tile_rows // block_rows, dtype=jnp.int32) * block_rows
    return lax.map(tile_block, starts).reshape(tile_rows, tile_cols, pair_width)


def block_update(activations, first_matrix, second_matrix, final_matrix, offset_vector):
    local_sequences, sequence_positions, feature_number = activations.shape
    row_count = lax.axis_size("row")
    col_count = lax.axis_size("col")
    row_block = sequence_positions // row_count
    col_block = sequence_positions // col_count
    hidden = first_matrix.shape[1]
    unrolled_products = standardize_features(activations).reshape(
        local_sequences * sequence_positions, feature_number
    )
    first_factor = jnp.dot(
        unrolled_products, first_matrix, preferred_element_type=jnp.float32
    ).astype(jnp.bfloat16)
    second_factor = jnp.dot(
        unrolled_products, second_matrix, preferred_element_type=jnp.float32
    ).astype(jnp.bfloat16)
    col_place = lax.axis_index("col")
    halves = second_factor.reshape(local_sequences, col_count, col_block * hidden)
    own_half = lax.dynamic_index_in_dim(halves, col_place, 1, keepdims=False)
    left_send = first_factor.reshape(local_sequences, row_count, row_block * hidden)
    left_got = lax.all_to_all(left_send, "row", split_axis=1, concat_axis=0, tiled=True)
    left_tile = left_got.reshape(-1, row_block, hidden)
    panel = lax.all_gather(own_half, "row", axis=0, tiled=True)
    right_tile = panel.reshape(-1, col_block, hidden)
    return pair_tiles(left_tile, right_tile, final_matrix, offset_vector)


def collective_body(activations, first_matrix, second_matrix, final_matrix, offsets):
    results = []
    for layer in range(activations.shape[0]):
        results.append(
            block_update(
                activations[layer],
                first_matrix[layer],
                second_matrix[layer],
                final_matrix[layer],
                offsets[layer],
            )
        )
    return jnp.stack(results, axis=0)


def dot32(a, b):
    return jnp.dot(a, b, preferred_element_type=jnp.float32)


def dot32_nt(a, b):
    return lax.dot_general(a, b, (((1,), (1,)), ((), ())), preferred_element_type=jnp.float32)


def opm_kernel(
    n,
    x_hbm,
    w1_hbm,
    w2_hbm,
    wf_hbm,
    b_hbm,
    out_hbm,
    x_ref,
    w1_ref,
    w2_ref,
    wf_ref,
    b_ref,
    normed,
    left_send,
    right_send,
    left_got,
    right_got,
    wide,
    w_rows,
    left_rows,
    right_rows,
    half_done,
    out_ref,
    in_sem,
    out_sem,
    left_ssem,
    left_rsem,
    right_ssem,
    right_rsem,
):
    layers, seqs, positions, _ = x_ref.shape
    hidden = w1_ref.shape[1]
    row_block, col_block = out_ref.shape[1], out_ref.shape[2]
    depth = n * seqs
    pairs = seqs // 2
    me = lax.axis_index("row")
    col = lax.axis_index("col")

    barrier = pltpu.get_barrier_semaphore()
    for step in range(1, n):
        pl.semaphore_signal(
            barrier,
            inc=1,
            device_id={"row": lax.rem(me + step, n)},
            device_id_type=pl.DeviceIdType.MESH,
        )

    fetches = []
    for layer in range(layers):
        fetches.append((x_hbm.at[layer], x_ref.at[layer]))
    fetches += [(w1_hbm, w1_ref), (w2_hbm, w2_ref), (wf_hbm, wf_ref), (b_hbm, b_ref)]
    fetches = [
        pltpu.make_async_copy(source, target, in_sem.at[k])
        for k, (source, target) in enumerate(fetches)
    ]
    for fetch in fetches:
        fetch.start()
    w1_fetch, w2_fetch, wf_fetch, b_fetch = fetches[layers:]

    def send(source, target, send_sem, recv_sem, to):
        copy = pltpu.make_async_remote_copy(
            src_ref=source,
            dst_ref=target,
            send_sem=send_sem,
            recv_sem=recv_sem,
            device_id={"row": to},
            device_id_type=pl.DeviceIdType.MESH,
        )
        copy.start()
        copies.append(copy)

    def arrived(buffer, recv_sem, layer, source):
        pltpu.make_async_remote_copy(
            src_ref=buffer.at[layer, source],
            dst_ref=buffer.at[layer, source],
            send_sem=left_ssem.at[layer, 0],
            recv_sem=recv_sem.at[layer, source],
            device_id={"row": source},
            device_id_type=pl.DeviceIdType.MESH,
        ).wait_recv()

    partner = me + 1 - 2 * lax.rem(me, 2)
    peers = [lax.rem(me + 2 * k, n) for k in range(1, n // 2)]
    others = [lax.rem(partner + 2 * k, n) for k in range(n // 2)]

    copies = []
    for layer in range(layers):
        fetches[layer].wait()
        if layer == 0:
            w1_fetch.wait()
            w2_fetch.wait()
        w1_wide = jnp.concatenate([w1_ref[layer]] * seqs, axis=0)
        w2_turned = w2_ref[layer]
        lane = lax.broadcasted_iota(jnp.int32, (positions, LANES), 1)
        packed = jnp.zeros((positions, LANES), jnp.float32)
        for s in range(seqs):
            entry = standardize_features(x_ref[layer, s])
            normed[s] = entry
            group = (lane >= s * hidden) & (lane < (s + 1) * hidden)
            packed = jnp.where(group, dot32_nt(entry, w1_wide), packed)
        left_send[layer] = packed.astype(jnp.bfloat16)
        mine = pl.ds(pl.multiple_of(col * col_block, col_block), col_block)
        for low in range(pairs):
            both = jnp.concatenate([normed[low, mine, :], normed[low + pairs, mine, :]], axis=0)
            right = dot32_nt(w2_turned, both).astype(jnp.bfloat16)
            right_send[layer, low * hidden : (low + 1) * hidden, :] = right
        own_rows = pl.ds(pl.multiple_of(me * row_block, row_block), row_block)
        left_got[layer, me] = left_send[layer, own_rows, :]
        right_got[layer, me] = right_send[layer]
        if layer == 0:
            pl.semaphore_wait(barrier, n - 1)
        for step in range(1, n):
            to = lax.rem(me + step, n)
            their_rows = pl.ds(pl.multiple_of(to * row_block, row_block), row_block)
            send(
                left_send.at[layer, their_rows, :],
                left_got.at[layer, me],
                left_ssem.at[layer, step],
                left_rsem.at[layer, me],
                to,
            )
        for step, to in enumerate(peers + [partner]):
            send(
                right_send.at[layer],
                right_got.at[layer, me],
                right_ssem.at[layer, step],
                right_rsem.at[layer, me],
                to,
            )

    wf_fetch.wait()
    b_fetch.wait()
    for layer in range(layers):
        wide[...] = wf_ref[layer].astype(jnp.float32)
        for d in range(hidden):
            piece = wide[pl.ds(d, hidden, stride=hidden), :].astype(jnp.bfloat16)
            for s in range(seqs):
                w_rows[layer, s * hidden : (s + 1) * hidden, d * LANES : (d + 1) * LANES] = piece

    lane = lax.broadcasted_iota(jnp.int32, (row_block, LANES), 1)
    stores = []
    for layer in range(layers):
        for step, source in enumerate(peers):
            arrived(right_got, right_rsem, layer, source)
            send(
                right_got.at[layer, source],
                right_got.at[layer, source],
                right_ssem.at[layer, n // 2 + step],
                right_rsem.at[layer, source],
                partner,
            )
        for step in range(1, n):
            arrived(left_got, left_rsem, layer, lax.rem(me + n - step, n))
        for r in range(n):
            block = left_got[layer, r].astype(jnp.float32)
            for s in range(seqs):
                group = (lane >= s * hidden) & (lane < (s + 1) * hidden)
                left_rows[pl.ds(r * seqs + s, row_block, stride=depth), :] = jnp.where(
                    group, block, 0.0
                )
        left_all = left_rows[...].astype(jnp.bfloat16)
        for d in range(0, hidden, 2):
            two = dot32(left_all, w_rows[layer, :, d * LANES : (d + 2) * LANES])
            two = two.astype(jnp.bfloat16)
            for k in range(2):
                for i in range(row_block):
                    half_done[
                        layer, (d + k) * depth : (d + k + 1) * depth, i * LANES : (i + 1) * LANES
                    ] = two[i * depth : (i + 1) * depth, k * LANES : (k + 1) * LANES]

    for layer in range(layers):
        for source in others:
            arrived(right_got, right_rsem, layer, source)
        for r in range(n):
            for low in range(pairs):
                block = right_got[layer, r, low * hidden : (low + 1) * hidden, :]
                block = block.astype(jnp.float32)
                right_rows[pl.ds(r * seqs + low, hidden, stride=depth), :] = block
                right_rows[pl.ds(r * seqs + low + pairs, hidden, stride=depth), :] = pltpu.roll(
                    block, col_block, 1
                )
        right_all = right_rows[...].T[:col_block].astype(jnp.bfloat16)
        scale = 1.0 / depth
        for i in range(0, row_block, 2):
            two = dot32(right_all, half_done[layer, :, i * LANES : (i + 2) * LANES]) * scale
            for k in range(2):
                done = two[:, k * LANES : (k + 1) * LANES] + b_ref[layer : layer + 1, :]
                out_ref[layer, i + k] = done.astype(jnp.bfloat16)
        store = pltpu.make_async_copy(out_ref.at[layer], out_hbm.at[layer], out_sem.at[layer])
        store.start()
        stores.append(store)

    for copy in copies:
        copy.wait_send()
    for store in stores:
        store.wait()


def kernel_fits(n, cols, x_shape, hidden, pair_width):
    layers, seqs, positions, features = x_shape
    row_block, col_block = positions // n, positions // cols
    depth = n * seqs
    need = layers * 4 * seqs * positions * features
    need += layers * 4 * depth * hidden * row_block * pair_width
    return (
        seqs * hidden == LANES
        and seqs % 2 == 0
        and 2 * col_block == LANES
        and pair_width == LANES
        and row_block % 16 == 0
        and depth % 16 == 0
        and n > 1
        and n % 2 == 0
        and need < VMEM_BUDGET
    )


def kernel_body(n, cols, x, w1, w2, wf, b):
    layers, seqs, positions, features = x.shape
    hidden = w1.shape[2]
    pair_width = wf.shape[2]
    row_block, col_block = positions // n, positions // cols
    depth = n * seqs
    packed = (seqs // 2) * hidden
    bf16, f32 = jnp.bfloat16, jnp.float32
    hbm = pl.BlockSpec(memory_space=pltpu.HBM)
    out_shape = (layers, row_block, col_block, pair_width)
    return pl.pallas_call(
        functools.partial(opm_kernel, n),
        out_shape=jax.ShapeDtypeStruct(out_shape, bf16),
        in_specs=[hbm] * 5,
        out_specs=hbm,
        scratch_shapes=[
            pltpu.VMEM(x.shape, bf16),
            pltpu.VMEM((layers, hidden, features), bf16),
            pltpu.VMEM((layers, hidden, features), bf16),
            pltpu.VMEM(wf.shape, bf16),
            pltpu.VMEM(b.shape, f32),
            pltpu.VMEM((seqs, positions, features), bf16),
            pltpu.VMEM((layers, positions, LANES), bf16),
            pltpu.VMEM((layers, packed, LANES), bf16),
            pltpu.VMEM((layers, n, row_block, LANES), bf16),
            pltpu.VMEM((layers, n, packed, LANES), bf16),
            pltpu.VMEM((hidden * hidden, pair_width), f32),
            pltpu.VMEM((layers, LANES, hidden * pair_width), bf16),
            pltpu.VMEM((row_block * depth, LANES), f32),
            pltpu.VMEM((hidden * depth, LANES), f32),
            pltpu.VMEM((layers, hidden * depth, row_block * pair_width), bf16),
            pltpu.VMEM(out_shape, bf16),
            pltpu.SemaphoreType.DMA((layers + 4,)),
            pltpu.SemaphoreType.DMA((layers,)),
            pltpu.SemaphoreType.DMA((layers, n)),
            pltpu.SemaphoreType.DMA((layers, n)),
            pltpu.SemaphoreType.DMA((layers, n)),
            pltpu.SemaphoreType.DMA((layers, n)),
        ],
        compiler_params=pltpu.CompilerParams(
            collective_id=0, has_side_effects=True, vmem_limit_bytes=VMEM_BUDGET
        ),
        name="outer_product_mean",
    )(x, jnp.swapaxes(w1, 1, 2), jnp.swapaxes(w2, 1, 2), wf, b)


def solution(mesh):
    n, cols = mesh.shape["row"], mesh.shape["col"]

    def body(x, w1, w2, wf, b):
        if kernel_fits(n, cols, x.shape, w1.shape[2], wf.shape[2]):
            return kernel_body(n, cols, x, w1, w2, wf, b)
        return collective_body(x, w1, w2, wf, b)

    in_specs = (P(None, ("grp", "row"), None, None), P(), P(), P(), P())
    out_specs = P(None, ("grp", "row"), "col", None)
    return jax.shard_map(body, mesh=mesh, in_specs=in_specs, out_specs=out_specs, check_vma=False)
```

```python
import functools

import jax
import jax.numpy as jnp
from jax import lax
from jax.experimental import pallas as pl
from jax.experimental.pallas import tpu as pltpu
from jax.sharding import PartitionSpec as P

LANES = 128
VMEM_BUDGET = 63 * 1024 * 1024


def standardize_features(activations):
    entry_lines = activations.astype(jnp.float32)
    average = jnp.mean(entry_lines, axis=-1, keepdims=True)
    centred = entry_lines - average
    variance = jnp.mean(centred * centred, axis=-1, keepdims=True)
    return (centred * lax.rsqrt(variance + 1e-05)).astype(jnp.bfloat16)


def pair_tiles(left_tile, right_tile, final_matrix, offset_vector):
    depth_all = left_tile.shape[0]
    tile_rows = left_tile.shape[1]
    tile_cols = right_tile.shape[1]
    hidden = left_tile.shape[2]
    pair_width = final_matrix.shape[1]
    block_rows = max(1, min(tile_rows, 2048 // tile_cols))
    reciprocal = 1.0 / depth_all

    def tile_block(offset):
        left_block = lax.dynamic_slice_in_dim(left_tile, offset, block_rows, 1)
        products = (
            jnp.einsum("sic,sjd->ijcd", left_block, right_tile, preferred_element_type=jnp.float32)
            * reciprocal
        )
        products = products.astype(jnp.bfloat16).reshape(block_rows * tile_cols, hidden * hidden)
        projected = (
            jnp.dot(products, final_matrix, preferred_element_type=jnp.float32) + offset_vector
        )
        return projected.astype(jnp.bfloat16).reshape(block_rows, tile_cols, pair_width)

    starts = jnp.arange(tile_rows // block_rows, dtype=jnp.int32) * block_rows
    return lax.map(tile_block, starts).reshape(tile_rows, tile_cols, pair_width)


def block_update(activations, first_matrix, second_matrix, final_matrix, offset_vector):
    local_sequences, sequence_positions, feature_number = activations.shape
    row_count = lax.axis_size("row")
    col_count = lax.axis_size("col")
    row_block = sequence_positions // row_count
    col_block = sequence_positions // col_count
    hidden = first_matrix.shape[1]
    unrolled_products = standardize_features(activations).reshape(
        local_sequences * sequence_positions, feature_number
    )
    first_factor = jnp.dot(
        unrolled_products, first_matrix, preferred_element_type=jnp.float32
    ).astype(jnp.bfloat16)
    second_factor = jnp.dot(
        unrolled_products, second_matrix, preferred_element_type=jnp.float32
    ).astype(jnp.bfloat16)
    col_place = lax.axis_index("col")
    halves = second_factor.reshape(local_sequences, col_count, col_block * hidden)
    own_half = lax.dynamic_index_in_dim(halves, col_place, 1, keepdims=False)
    left_send = first_factor.reshape(local_sequences, row_count, row_block * hidden)
    left_got = lax.all_to_all(left_send, "row", split_axis=1, concat_axis=0, tiled=True)
    left_tile = left_got.reshape(-1, row_block, hidden)
    panel = lax.all_gather(own_half, "row", axis=0, tiled=True)
    right_tile = panel.reshape(-1, col_block, hidden)
    return pair_tiles(left_tile, right_tile, final_matrix, offset_vector)


def collective_body(activations, first_matrix, second_matrix, final_matrix, offsets):
    results = []
    for layer in range(activations.shape[0]):
        results.append(
            block_update(
                activations[layer],
                first_matrix[layer],
                second_matrix[layer],
                final_matrix[layer],
                offsets[layer],
            )
        )
    return jnp.stack(results, axis=0)


def dot32(a, b):
    return jnp.dot(a, b, preferred_element_type=jnp.float32)


def dot32_nt(a, b):
    return lax.dot_general(a, b, (((1,), (1,)), ((), ())), preferred_element_type=jnp.float32)


def opm_kernel(
    n,
    x_hbm,
    w1_hbm,
    w2_hbm,
    wf_hbm,
    b_hbm,
    out_hbm,
    x_ref,
    w1_ref,
    w2_ref,
    wf_ref,
    b_ref,
    normed,
    left_send,
    right_send,
    left_got,
    right_got,
    wide,
    w_rows,
    left_rows,
    right_rows,
    half_done,
    near,
    out_ref,
    in_sem,
    out_sem,
    left_ssem,
    left_rsem,
    right_ssem,
    right_rsem,
):
    layers, seqs, positions, _ = x_ref.shape
    hidden = w1_ref.shape[1]
    row_block, col_block = out_ref.shape[1], out_ref.shape[2]
    depth = n * seqs
    half = depth // 2
    pairs = seqs // 2
    me = lax.axis_index("row")
    col = lax.axis_index("col")

    barrier = pltpu.get_barrier_semaphore()
    for step in range(1, n):
        pl.semaphore_signal(
            barrier,
            inc=1,
            device_id={"row": lax.rem(me + step, n)},
            device_id_type=pl.DeviceIdType.MESH,
        )

    fetches = []
    for layer in range(layers):
        fetches.append((x_hbm.at[layer], x_ref.at[layer]))
    fetches += [(w1_hbm, w1_ref), (w2_hbm, w2_ref), (wf_hbm, wf_ref), (b_hbm, b_ref)]
    fetches = [
        pltpu.make_async_copy(source, target, in_sem.at[k])
        for k, (source, target) in enumerate(fetches)
    ]
    for fetch in fetches:
        fetch.start()
    w1_fetch, w2_fetch, wf_fetch, b_fetch = fetches[layers:]

    def send(source, target, send_sem, recv_sem, to):
        copy = pltpu.make_async_remote_copy(
            src_ref=source,
            dst_ref=target,
            send_sem=send_sem,
            recv_sem=recv_sem,
            device_id={"row": to},
            device_id_type=pl.DeviceIdType.MESH,
        )
        copy.start()
        copies.append(copy)

    def arrived(buffer, recv_sem, layer, source):
        pltpu.make_async_remote_copy(
            src_ref=buffer.at[layer, source],
            dst_ref=buffer.at[layer, source],
            send_sem=left_ssem.at[layer, 0],
            recv_sem=recv_sem.at[layer, source],
            device_id={"row": source},
            device_id_type=pl.DeviceIdType.MESH,
        ).wait_recv()

    partner = me + 1 - 2 * lax.rem(me, 2)
    peers = [lax.rem(me + 2 * k, n) for k in range(1, n // 2)]
    others = [lax.rem(partner + 2 * k, n) for k in range(n // 2)]

    copies = []
    for layer in range(layers):
        fetches[layer].wait()
        if layer == 0:
            w1_fetch.wait()
            w2_fetch.wait()
        w1_wide = jnp.concatenate([w1_ref[layer]] * seqs, axis=0)
        w2_turned = w2_ref[layer]
        lane = lax.broadcasted_iota(jnp.int32, (positions, LANES), 1)
        packed = jnp.zeros((positions, LANES), jnp.float32)
        for s in range(seqs):
            entry = standardize_features(x_ref[layer, s])
            normed[s] = entry
            group = (lane >= s * hidden) & (lane < (s + 1) * hidden)
            packed = jnp.where(group, dot32_nt(entry, w1_wide), packed)
        left_send[layer] = packed.astype(jnp.bfloat16)
        mine = pl.ds(pl.multiple_of(col * col_block, col_block), col_block)
        for low in range(pairs):
            both = jnp.concatenate([normed[low, mine, :], normed[low + pairs, mine, :]], axis=0)
            right = dot32_nt(w2_turned, both).astype(jnp.bfloat16)
            right_send[layer, low * hidden : (low + 1) * hidden, :] = right
        own_rows = pl.ds(pl.multiple_of(me * row_block, row_block), row_block)
        left_got[layer, me] = left_send[layer, own_rows, :]
        right_got[layer, me] = right_send[layer]
        if layer == 0:
            pl.semaphore_wait(barrier, n - 1)
        for step in range(1, n):
            to = lax.rem(me + step, n)
            their_rows = pl.ds(pl.multiple_of(to * row_block, row_block), row_block)
            send(
                left_send.at[layer, their_rows, :],
                left_got.at[layer, me],
                left_ssem.at[layer, step],
                left_rsem.at[layer, me],
                to,
            )
        for step, to in enumerate(peers + [partner]):
            send(
                right_send.at[layer],
                right_got.at[layer, me],
                right_ssem.at[layer, step],
                right_rsem.at[layer, me],
                to,
            )

    wf_fetch.wait()
    b_fetch.wait()
    for layer in range(layers):
        wide[...] = wf_ref[layer].astype(jnp.float32)
        for d in range(hidden):
            piece = wide[pl.ds(d, hidden, stride=hidden), :].astype(jnp.bfloat16)
            for s in range(seqs):
                w_rows[layer, s * hidden : (s + 1) * hidden, d * LANES : (d + 1) * LANES] = piece

    lane = lax.broadcasted_iota(jnp.int32, (row_block, LANES), 1)
    stores = []
    for layer in range(layers):
        for step, source in enumerate(peers):
            arrived(right_got, right_rsem, layer, source)
            send(
                right_got.at[layer, source],
                right_got.at[layer, source],
                right_ssem.at[layer, n // 2 + step],
                right_rsem.at[layer, source],
                partner,
            )
        for step in range(1, n):
            arrived(left_got, left_rsem, layer, lax.rem(me + n - step, n))
        for r, source in enumerate([me] + peers + others):
            block = left_got[layer, source].astype(jnp.float32)
            for s in range(seqs):
                group = (lane >= s * hidden) & (lane < (s + 1) * hidden)
                left_rows[pl.ds(r * seqs + s, row_block, stride=depth), :] = jnp.where(
                    group, block, 0.0
                )
        left_all = left_rows[...].astype(jnp.bfloat16)
        for d in range(0, hidden, 2):
            weights = w_rows[layer, :, d * LANES : (d + 2) * LANES]
            for first in range(0, row_block, 4):
                rows = left_all[first * depth : (first + 4) * depth]
                two = dot32(rows, weights).astype(jnp.bfloat16)
                for k in range(2):
                    for i in range(4):
                        for g in range(2):
                            at = (g * hidden + d + k) * half
                            half_done[
                                layer, at : at + half, (first + i) * LANES : (first + i + 1) * LANES
                            ] = two[
                                i * depth + g * half : i * depth + (g + 1) * half,
                                k * LANES : (k + 1) * LANES,
                            ]

    def right_side(layer, sources):
        for r, source in enumerate(sources):
            for low in range(pairs):
                block = right_got[layer, source, low * hidden : (low + 1) * hidden, :]
                block = block.astype(jnp.float32)
                right_rows[pl.ds(r * seqs + low, hidden, stride=half), :] = block
                right_rows[pl.ds(r * seqs + low + pairs, hidden, stride=half), :] = pltpu.roll(
                    block, col_block, 1
                )
        return right_rows[...].T[:col_block].astype(jnp.bfloat16)

    for layer in range(layers):
        right_near = right_side(layer, [me] + peers)
        for i in range(0, row_block, 2):
            lanes = slice(i * LANES, (i + 2) * LANES)
            near[layer, :, lanes] = dot32(right_near, half_done[layer, : hidden * half, lanes])
    scale = 1.0 / depth
    for layer in range(layers):
        for source in others:
            arrived(right_got, right_rsem, layer, source)
        right_far = right_side(layer, others)
        for i in range(0, row_block, 2):
            lanes = slice(i * LANES, (i + 2) * LANES)
            two = dot32(right_far, half_done[layer, hidden * half :, lanes])
            two = (two + near[layer, :, lanes]) * scale
            for k in range(2):
                done = two[:, k * LANES : (k + 1) * LANES] + b_ref[layer : layer + 1, :]
                out_ref[layer, i + k] = done.astype(jnp.bfloat16)
        store = pltpu.make_async_copy(out_ref.at[layer], out_hbm.at[layer], out_sem.at[layer])
        store.start()
        stores.append(store)

    for copy in copies:
        copy.wait_send()
    for store in stores:
        store.wait()


def kernel_fits(n, cols, x_shape, hidden, pair_width):
    layers, seqs, positions, features = x_shape
    row_block, col_block = positions // n, positions // cols
    depth = n * seqs
    need = layers * 4 * seqs * positions * features
    need += layers * 4 * depth * hidden * row_block * pair_width
    return (
        seqs * hidden == LANES
        and seqs % 2 == 0
        and 2 * col_block == LANES
        and pair_width == LANES
        and row_block % 16 == 0
        and depth % 32 == 0
        and n > 1
        and n % 2 == 0
        and need < VMEM_BUDGET
    )


def kernel_body(n, cols, x, w1, w2, wf, b):
    layers, seqs, positions, features = x.shape
    hidden = w1.shape[2]
    pair_width = wf.shape[2]
    row_block, col_block = positions // n, positions // cols
    depth = n * seqs
    packed = (seqs // 2) * hidden
    bf16, f32 = jnp.bfloat16, jnp.float32
    hbm = pl.BlockSpec(memory_space=pltpu.HBM)
    out_shape = (layers, row_block, col_block, pair_width)
    return pl.pallas_call(
        functools.partial(opm_kernel, n),
        out_shape=jax.ShapeDtypeStruct(out_shape, bf16),
        in_specs=[hbm] * 5,
        out_specs=hbm,
        scratch_shapes=[
            pltpu.VMEM(x.shape, bf16),
            pltpu.VMEM((layers, hidden, features), bf16),
            pltpu.VMEM((layers, hidden, features), bf16),
            pltpu.VMEM(wf.shape, bf16),
            pltpu.VMEM(b.shape, f32),
            pltpu.VMEM((seqs, positions, features), bf16),
            pltpu.VMEM((layers, positions, LANES), bf16),
            pltpu.VMEM((layers, packed, LANES), bf16),
            pltpu.VMEM((layers, n, row_block, LANES), bf16),
            pltpu.VMEM((layers, n, packed, LANES), bf16),
            pltpu.VMEM((hidden * hidden, pair_width), f32),
            pltpu.VMEM((layers, LANES, hidden * pair_width), bf16),
            pltpu.VMEM((row_block * depth, LANES), f32),
            pltpu.VMEM((hidden * depth // 2, LANES), f32),
            pltpu.VMEM((layers, hidden * depth, row_block * pair_width), bf16),
            pltpu.VMEM((layers, col_block, row_block * pair_width), f32),
            pltpu.VMEM(out_shape, bf16),
            pltpu.SemaphoreType.DMA((layers + 4,)),
            pltpu.SemaphoreType.DMA((layers,)),
            pltpu.SemaphoreType.DMA((layers, n)),
            pltpu.SemaphoreType.DMA((layers, n)),
            pltpu.SemaphoreType.DMA((layers, n)),
            pltpu.SemaphoreType.DMA((layers, n)),
        ],
        compiler_params=pltpu.CompilerParams(
            collective_id=0, has_side_effects=True, vmem_limit_bytes=VMEM_BUDGET
        ),
        name="outer_product_mean",
    )(x, jnp.swapaxes(w1, 1, 2), jnp.swapaxes(w2, 1, 2), wf, b)


def solution(mesh):
    n, cols = mesh.shape["row"], mesh.shape["col"]

    def body(x, w1, w2, wf, b):
        if kernel_fits(n, cols, x.shape, w1.shape[2], wf.shape[2]):
            return kernel_body(n, cols, x, w1, w2, wf, b)
        return collective_body(x, w1, w2, wf, b)

    in_specs = (P(None, ("grp", "row"), None, None), P(), P(), P(), P())
    out_specs = P(None, ("grp", "row"), "col", None)
    return jax.shard_map(body, mesh=mesh, in_specs=in_specs, out_specs=out_specs, check_vma=False)
```

```python
import functools

import jax
import jax.numpy as jnp
from jax import lax
from jax.experimental import pallas as pl
from jax.experimental.pallas import tpu as pltpu
from jax.sharding import PartitionSpec as P

LANES = 128
VMEM_BUDGET = (64 * 1024 - 11200) * 1024


def standardize_features(activations):
    entry_lines = activations.astype(jnp.float32)
    average = jnp.mean(entry_lines, axis=-1, keepdims=True)
    centred = entry_lines - average
    variance = jnp.mean(centred * centred, axis=-1, keepdims=True)
    return (centred * lax.rsqrt(variance + 1e-05)).astype(jnp.bfloat16)


def pair_tiles(left_tile, right_tile, final_matrix, offset_vector):
    depth_all = left_tile.shape[0]
    tile_rows = left_tile.shape[1]
    tile_cols = right_tile.shape[1]
    hidden = left_tile.shape[2]
    pair_width = final_matrix.shape[1]
    block_rows = max(1, min(tile_rows, 2048 // tile_cols))
    reciprocal = 1.0 / depth_all

    def tile_block(offset):
        left_block = lax.dynamic_slice_in_dim(left_tile, offset, block_rows, 1)
        products = (
            jnp.einsum("sic,sjd->ijcd", left_block, right_tile, preferred_element_type=jnp.float32)
            * reciprocal
        )
        products = products.astype(jnp.bfloat16).reshape(block_rows * tile_cols, hidden * hidden)
        projected = (
            jnp.dot(products, final_matrix, preferred_element_type=jnp.float32) + offset_vector
        )
        return projected.astype(jnp.bfloat16).reshape(block_rows, tile_cols, pair_width)

    starts = jnp.arange(tile_rows // block_rows, dtype=jnp.int32) * block_rows
    return lax.map(tile_block, starts).reshape(tile_rows, tile_cols, pair_width)


def block_update(activations, first_matrix, second_matrix, final_matrix, offset_vector):
    local_sequences, sequence_positions, feature_number = activations.shape
    row_count = lax.axis_size("row")
    col_count = lax.axis_size("col")
    row_block = sequence_positions // row_count
    col_block = sequence_positions // col_count
    hidden = first_matrix.shape[1]
    unrolled_products = standardize_features(activations).reshape(
        local_sequences * sequence_positions, feature_number
    )
    first_factor = jnp.dot(
        unrolled_products, first_matrix, preferred_element_type=jnp.float32
    ).astype(jnp.bfloat16)
    second_factor = jnp.dot(
        unrolled_products, second_matrix, preferred_element_type=jnp.float32
    ).astype(jnp.bfloat16)
    col_place = lax.axis_index("col")
    halves = second_factor.reshape(local_sequences, col_count, col_block * hidden)
    own_half = lax.dynamic_index_in_dim(halves, col_place, 1, keepdims=False)
    left_send = first_factor.reshape(local_sequences, row_count, row_block * hidden)
    left_got = lax.all_to_all(left_send, "row", split_axis=1, concat_axis=0, tiled=True)
    left_tile = left_got.reshape(-1, row_block, hidden)
    panel = lax.all_gather(own_half, "row", axis=0, tiled=True)
    right_tile = panel.reshape(-1, col_block, hidden)
    return pair_tiles(left_tile, right_tile, final_matrix, offset_vector)


def collective_body(activations, first_matrix, second_matrix, final_matrix, offsets):
    results = []
    for layer in range(activations.shape[0]):
        results.append(
            block_update(
                activations[layer],
                first_matrix[layer],
                second_matrix[layer],
                final_matrix[layer],
                offsets[layer],
            )
        )
    return jnp.stack(results, axis=0)


def dot32(a, b):
    return jnp.dot(a, b, preferred_element_type=jnp.float32)


def dot32_nt(a, b):
    return lax.dot_general(a, b, (((1,), (1,)), ((), ())), preferred_element_type=jnp.float32)


def opm_kernel(
    n,
    x_hbm,
    small_ref,
    wf_hbm,
    out_hbm,
    x_ref,
    wf_ref,
    normed,
    left_send,
    right_send,
    left_got,
    right_got,
    wide,
    w_rows,
    left_rows,
    right_rows,
    half_done,
    near,
    out_ref,
    in_sem,
    out_sem,
    left_ssem,
    left_rsem,
    right_ssem,
    right_rsem,
):
    layers, seqs, positions, _ = x_ref.shape
    hidden = LANES // seqs
    row_block, col_block = out_ref.shape[1], out_ref.shape[2]
    depth = n * seqs
    half = depth // 2
    pairs = seqs // 2
    me = lax.axis_index("row")
    col = lax.axis_index("col")

    barrier = pltpu.get_barrier_semaphore()
    for step in range(1, n):
        pl.semaphore_signal(
            barrier,
            inc=1,
            device_id={"row": lax.rem(me + step, n)},
            device_id_type=pl.DeviceIdType.MESH,
        )

    fetches = []
    for layer in range(layers):
        fetches.append((x_hbm.at[layer], x_ref.at[layer]))
    fetches.append((wf_hbm, wf_ref))
    fetches = [
        pltpu.make_async_copy(source, target, in_sem.at[k])
        for k, (source, target) in enumerate(fetches)
    ]
    for fetch in fetches:
        fetch.start()
    wf_fetch = fetches[layers]

    def send(source, target, send_sem, recv_sem, to):
        copy = pltpu.make_async_remote_copy(
            src_ref=source,
            dst_ref=target,
            send_sem=send_sem,
            recv_sem=recv_sem,
            device_id={"row": to},
            device_id_type=pl.DeviceIdType.MESH,
        )
        copy.start()
        copies.append(copy)

    def arrived(buffer, recv_sem, layer, source):
        pltpu.make_async_remote_copy(
            src_ref=buffer.at[layer, source],
            dst_ref=buffer.at[layer, source],
            send_sem=left_ssem.at[layer, 0],
            recv_sem=recv_sem.at[layer, source],
            device_id={"row": source},
            device_id_type=pl.DeviceIdType.MESH,
        ).wait_recv()

    partner = me + 1 - 2 * lax.rem(me, 2)
    peers = [lax.rem(me + 2 * k, n) for k in range(1, n // 2)]
    others = [lax.rem(partner + 2 * k, n) for k in range(n // 2)]

    copies = []
    for layer in range(layers):
        fetches[layer].wait()
        w1_wide = jnp.concatenate([small_ref[layer, :hidden].astype(jnp.bfloat16)] * seqs, axis=0)
        w2_turned = small_ref[layer, hidden : 2 * hidden].astype(jnp.bfloat16)
        lane = lax.broadcasted_iota(jnp.int32, (positions, LANES), 1)
        packed = jnp.zeros((positions, LANES), jnp.float32)
        for s in range(seqs):
            entry = standardize_features(x_ref[layer, s])
            normed[s] = entry
            group = (lane >= s * hidden) & (lane < (s + 1) * hidden)
            packed = jnp.where(group, dot32_nt(entry, w1_wide), packed)
        left_send[layer] = packed.astype(jnp.bfloat16)
        mine = pl.ds(pl.multiple_of(col * col_block, col_block), col_block)
        for low in range(pairs):
            both = jnp.concatenate([normed[low, mine, :], normed[low + pairs, mine, :]], axis=0)
            right = dot32_nt(w2_turned, both).astype(jnp.bfloat16)
            right_send[layer, low * hidden : (low + 1) * hidden, :] = right
        own_rows = pl.ds(pl.multiple_of(me * row_block, row_block), row_block)
        left_got[layer, me] = left_send[layer, own_rows, :]
        right_got[layer, me] = right_send[layer]
        if layer == 0:
            pl.semaphore_wait(barrier, n - 1)
        for step in range(1, n):
            to = lax.rem(me + step, n)
            their_rows = pl.ds(pl.multiple_of(to * row_block, row_block), row_block)
            send(
                left_send.at[layer, their_rows, :],
                left_got.at[layer, me],
                left_ssem.at[layer, step],
                left_rsem.at[layer, me],
                to,
            )
        for step, to in enumerate(peers + [partner]):
            send(
                right_send.at[layer],
                right_got.at[layer, me],
                right_ssem.at[layer, step],
                right_rsem.at[layer, me],
                to,
            )

    wf_fetch.wait()
    for layer in range(layers):
        wide[...] = wf_ref[layer].astype(jnp.float32)
        for d in range(hidden):
            piece = wide[pl.ds(d, hidden, stride=hidden), :].astype(jnp.bfloat16)
            for s in range(seqs):
                w_rows[layer, s * hidden : (s + 1) * hidden, d * LANES : (d + 1) * LANES] = piece

    lane = lax.broadcasted_iota(jnp.int32, (row_block, LANES), 1)
    stores = []
    for layer in range(layers):
        for step, source in enumerate(peers):
            arrived(right_got, right_rsem, layer, source)
            send(
                right_got.at[layer, source],
                right_got.at[layer, source],
                right_ssem.at[layer, n // 2 + step],
                right_rsem.at[layer, source],
                partner,
            )
        for step in range(1, n):
            arrived(left_got, left_rsem, layer, lax.rem(me + n - step, n))
        for r, source in enumerate([me] + peers + others):
            block = left_got[layer, source].astype(jnp.float32)
            for s in range(seqs):
                group = (lane >= s * hidden) & (lane < (s + 1) * hidden)
                left_rows[pl.ds(r * seqs + s, row_block, stride=depth), :] = jnp.where(
                    group, block, 0.0
                )
        left_all = left_rows[...].astype(jnp.bfloat16)
        for d in range(0, hidden, 2):
            weights = w_rows[layer, :, d * LANES : (d + 2) * LANES]
            for first in range(0, row_block, 4):
                rows = left_all[first * depth : (first + 4) * depth]
                two = dot32(rows, weights).astype(jnp.bfloat16)
                for k in range(2):
                    for i in range(4):
                        for g in range(2):
                            at = (g * hidden + d + k) * half
                            half_done[
                                layer, at : at + half, (first + i) * LANES : (first + i + 1) * LANES
                            ] = two[
                                i * depth + g * half : i * depth + (g + 1) * half,
                                k * LANES : (k + 1) * LANES,
                            ]

    def right_side(layer, sources):
        for r, source in enumerate(sources):
            for low in range(pairs):
                block = right_got[layer, source, low * hidden : (low + 1) * hidden, :]
                block = block.astype(jnp.float32)
                right_rows[pl.ds(r * seqs + low, hidden, stride=half), :] = block
                right_rows[pl.ds(r * seqs + low + pairs, hidden, stride=half), :] = pltpu.roll(
                    block, col_block, 1
                )
        return right_rows[...].T[:col_block].astype(jnp.bfloat16)

    for layer in range(layers):
        right_near = right_side(layer, [me] + peers)
        for i in range(0, row_block, 2):
            lanes = slice(i * LANES, (i + 2) * LANES)
            near[layer, :, lanes] = dot32(right_near, half_done[layer, : hidden * half, lanes])
    scale = 1.0 / depth
    for layer in range(layers):
        for source in others:
            arrived(right_got, right_rsem, layer, source)
        right_far = right_side(layer, others)
        for i in range(0, row_block, 2):
            lanes = slice(i * LANES, (i + 2) * LANES)
            two = dot32(right_far, half_done[layer, hidden * half :, lanes])
            two = (two + near[layer, :, lanes]) * scale
            for k in range(2):
                done = two[:, k * LANES : (k + 1) * LANES] + small_ref[layer, 2 * hidden : 2 * hidden + 1, :LANES]
                out_ref[layer, i + k] = done.astype(jnp.bfloat16)
        store = pltpu.make_async_copy(out_ref.at[layer], out_hbm.at[layer], out_sem.at[layer])
        store.start()
        stores.append(store)

    for copy in copies:
        copy.wait_send()
    for store in stores:
        store.wait()


def kernel_fits(n, cols, x_shape, hidden, pair_width):
    layers, seqs, positions, features = x_shape
    row_block, col_block = positions // n, positions // cols
    depth = n * seqs
    need = layers * 4 * seqs * positions * features
    need += layers * 4 * depth * hidden * row_block * pair_width
    return (
        seqs * hidden == LANES
        and seqs % 2 == 0
        and 2 * col_block == LANES
        and pair_width == LANES
        and row_block % 16 == 0
        and depth % 32 == 0
        and n > 1
        and n % 2 == 0
        and need < VMEM_BUDGET
    )


def kernel_body(n, cols, x, w1, w2, wf, b):
    layers, seqs, positions, features = x.shape
    hidden = w1.shape[2]
    pair_width = wf.shape[2]
    row_block, col_block = positions // n, positions // cols
    depth = n * seqs
    packed = (seqs // 2) * hidden
    bf16, f32 = jnp.bfloat16, jnp.float32
    hbm = pl.BlockSpec(memory_space=pltpu.HBM)
    out_shape = (layers, row_block, col_block, pair_width)
    offsets = jnp.pad(b[:, None, :], ((0, 0), (0, 7), (0, features - pair_width)))
    turned = [jnp.swapaxes(w, 1, 2).astype(f32) for w in (w1, w2)]
    small = jnp.concatenate(turned + [offsets], axis=1)
    return pl.pallas_call(
        functools.partial(opm_kernel, n),
        out_shape=jax.ShapeDtypeStruct(out_shape, bf16),
        in_specs=[hbm, pl.BlockSpec(memory_space=pltpu.VMEM), hbm],
        out_specs=hbm,
        scratch_shapes=[
            pltpu.VMEM(x.shape, bf16),
            pltpu.VMEM(wf.shape, bf16),
            pltpu.VMEM((seqs, positions, features), bf16),
            pltpu.VMEM((layers, positions, LANES), bf16),
            pltpu.VMEM((layers, packed, LANES), bf16),
            pltpu.VMEM((layers, n, row_block, LANES), bf16),
            pltpu.VMEM((layers, n, packed, LANES), bf16),
            pltpu.VMEM((hidden * hidden, pair_width), f32),
            pltpu.VMEM((layers, LANES, hidden * pair_width), bf16),
            pltpu.VMEM((row_block * depth, LANES), f32),
            pltpu.VMEM((hidden * depth // 2, LANES), f32),
            pltpu.VMEM((layers, hidden * depth, row_block * pair_width), bf16),
            pltpu.VMEM((layers, col_block, row_block * pair_width), f32),
            pltpu.VMEM(out_shape, bf16),
            pltpu.SemaphoreType.DMA((layers + 1,)),
            pltpu.SemaphoreType.DMA((layers,)),
            pltpu.SemaphoreType.DMA((layers, n)),
            pltpu.SemaphoreType.DMA((layers, n)),
            pltpu.SemaphoreType.DMA((layers, n)),
            pltpu.SemaphoreType.DMA((layers, n)),
        ],
        compiler_params=pltpu.CompilerParams(
            collective_id=0, has_side_effects=True, vmem_limit_bytes=VMEM_BUDGET
        ),
        name="outer_product_mean",
    )(x, small, wf)


def solution(mesh):
    n, cols = mesh.shape["row"], mesh.shape["col"]

    def body(x, w1, w2, wf, b):
        if kernel_fits(n, cols, x.shape, w1.shape[2], wf.shape[2]):
            return kernel_body(n, cols, x, w1, w2, wf, b)
        return collective_body(x, w1, w2, wf, b)

    in_specs = (P(None, ("grp", "row"), None, None), P(), P(), P(), P())
    out_specs = P(None, ("grp", "row"), "col", None)
    return jax.shard_map(body, mesh=mesh, in_specs=in_specs, out_specs=out_specs, check_vma=False)
```
